512 devices in a mesh: seq: 128 (over z, y_hi, x), chan: 4 (over y_lo, core).
Axes of the slice: x: 4, y: 8 (y_hi: 4, y_lo: 2; y = y_hi * 2 + y_lo), z: 8, core: 2. Of those that a mesh axis runs over, the one named last changes fastest.
Arguments:
- inputs: bfloat16 [262144, 512], P('seq', 'chan'), may hold values from -6 to 6
- gate: bfloat16 [262144, 512], P('seq', 'chan'), may hold values from -6 to 6
- cotangent: bfloat16 [262144, 512], P('seq', 'chan'), may hold values from -1.1953125 to 1.1953125
- right_factor: bfloat16 [512, 512, 512], P('seq', 'chan'), may hold values from -0.25 to 0.25
- left_factor: bfloat16 [512, 512, 512], P('seq', 'chan'), may hold values from -0.25 to 0.25
Outputs:
- input_grad: bfloat16 [262144, 512], P('seq', 'chan')
- gate_grad: bfloat16 [262144, 512], P('seq', 'chan')
- right_grad: bfloat16 [512, 512, 512], P('seq', 'chan')
- left_grad: bfloat16 [512, 512, 512], P('seq', 'chan')
The draws below stay inside these ranges and needn't reach their ends.
All inputs are finite; a program needn't handle non-finite values.
Results may differ from the reference program's by a relative error of at most 0.013.
Values may be sent and summed in bfloat16 or wider, within the bound.
A program may use at most 64 MiB of HBM per device.

```python
import jax
import jax.numpy as jnp
from jax import lax

N = 512
C = 512
TOKENS = 262144
N_CHAN = 4


def shard_levels(key, shape, cuts, smallest, high):
    def one(dim, parts):
        draws = jax.random.uniform(jax.random.fold_in(jax.random.fold_in(key, 6), dim), (parts,), jnp.float32, smallest / len(cuts), high / len(cuts))
        return jnp.repeat(jnp.exp(draws), shape[dim] // parts).reshape((-1,) + (1,) * (len(shape) - dim - 1))

    gain = one(*cuts[0])
    for cut in cuts[1:]:
        gain = gain * one(*cut)
    return gain


def bell_draw(key, dims, scale, reach, shards=(), held_as=jnp.bfloat16):
    values = scale * jax.random.normal(key, dims, jnp.float32)
    if shards:
        values = values * shard_levels(key, dims, shards, -0.22, 0.18)
    return jnp.clip(values, -reach, reach).astype(held_as)


def setup_inputs(seed: int = 0) -> dict:
    streams_of = jax.random.split(jax.random.key(seed), 6)
    inputs = bell_draw(streams_of[0], (TOKENS, C), 1.0, 6.0, ((0, 128), (1, 4)))
    gate = bell_draw(streams_of[1], (TOKENS, C), 1.0, 6.0, ((0, 128), (1, 4)))
    cotangent = bell_draw(streams_of[2], (TOKENS, C), 0.2, 1.1953125, ((0, 128), (1, 4)))
    right_factor = bell_draw(streams_of[3], (N, N, N), N ** -0.5, 0.25, ((0, 128), (1, 4)))
    left_factor = bell_draw(streams_of[4], (N, N, N), N ** -0.5, 0.25, ((0, 128), (1, 4)))
    return dict(inputs=inputs, gate=gate, cotangent=cotangent, right_factor=right_factor, left_factor=left_factor)


def grouped_sum(left_data, right_data, form):
    group = C // N_CHAN
    total = None
    for index in range(N_CHAN):
        lower_edge = index * group
        upper_edge = lower_edge + group
        term = jnp.einsum(form, left_data[:, :, lower_edge:upper_edge].astype(jnp.float32),
                          right_data[:, :, lower_edge:upper_edge].astype(jnp.float32))
        rounded = lax.optimization_barrier(term.astype(jnp.bfloat16)).astype(jnp.float32)
        total = rounded if total is None else total + rounded
    return total


def reference(inputs, gate, cotangent, right_factor, left_factor):
    grid_in = inputs.reshape(N, N, C)
    gate_grid = gate.reshape(N, N, C).astype(jnp.float32)
    cot_grid = cotangent.reshape(N, N, C).astype(jnp.float32)
    right_wide = right_factor.astype(jnp.float32)
    left_wide = left_factor.astype(jnp.float32)
    upper = jnp.einsum('ikj,ijc->ikc', right_wide, grid_in.astype(jnp.float32)).astype(jnp.bfloat16)
    mixed = jnp.einsum('kmi,ikc->mkc', left_wide, upper.astype(jnp.float32)).astype(jnp.bfloat16)
    gate_grad = (cot_grid * mixed.astype(jnp.float32)).astype(jnp.bfloat16)
    back = (cot_grid * gate_grid).astype(jnp.bfloat16)
    lower = jnp.einsum('kmi,mkc->ikc', left_wide, back.astype(jnp.float32)).astype(jnp.bfloat16)
    input_grad = jnp.einsum('ikj,ikc->ijc', right_wide, lower.astype(jnp.float32)).astype(jnp.bfloat16)
    left_grad = grouped_sum(back, upper, 'mkc,ikc->kmi').astype(jnp.bfloat16)
    right_grad = grouped_sum(lower, grid_in, 'ikc,ijc->ikj').astype(jnp.bfloat16)
    return (input_grad.reshape(N * N, C), gate_grad.reshape(N * N, C), right_grad, left_grad)
```

```python
import functools

import jax
import jax.numpy as jnp
from jax import lax
from jax.experimental import pallas as pl
from jax.experimental.pallas import tpu as pltpu
from jax.sharding import PartitionSpec as P

MESH = pl.DeviceIdType.MESH
BF16 = jnp.bfloat16
F32 = jnp.float32
LOADS = 5
UPPER, MIXED, BACK, LOWER = range(4)
RIGHT, LEFT = range(2)


def torus(n_seq):
    return {128: (8, 4, 4), 8: (2, 2, 2)}[n_seq]


def dot(a, b, dims=((1,), (0,))):
    return lax.dot_general(a, b, (dims, ((), ())), preferred_element_type=F32)


def kernel(
    n_seq,
    x_hbm, g_hbm, y_hbm, r_hbm, l_hbm,
    ig_hbm, gg_hbm, rg_hbm, lg_hbm,
    xv, gv, yv, fac, out_s, out_r, part, spread, flat,
    bk, uk, lk,
    ig, gg, near_s, near_r, home_s, home_r, far_s, far_r, far_f, home_f, grad,
    load_sem, a2a_send, a2a_recv, sib_send, sib_recv, par_send, par_recv, fwd_send, fwd_recv,
    near_ss, near_rs, home_ss, home_rs, far_ss, far_rs, out_sem, row_sem, plane_sem,
):
    zs, ys, xs = torus(n_seq)
    blocks, order, width = fac.shape[1], fac.shape[2], xv.shape[1]
    quarter = order // 4
    dests = n_seq // 4
    piece = 4 * blocks
    seq, ch = lax.axis_index("seq"), lax.axis_index("chan")
    z, y, x = seq // (ys * xs), (seq // xs) % ys, seq % xs
    sib, par = ch ^ 1, ch ^ 2

    def rows(start, size):
        return pl.ds(pl.multiple_of(start, size), size)

    mine = rows(ch * quarter, quarter)
    loads = [
        pltpu.make_async_copy(src, dst, load_sem.at[n])
        for n, (src, dst) in enumerate((
            (y_hbm, yv), (g_hbm, gv), (x_hbm, xv),
            (r_hbm, fac.at[RIGHT, :, mine, :]), (l_hbm, fac.at[LEFT, :, mine, :]),
        ))
    ]
    for load in loads:
        load.start()

    def seq_of(a, b, c):
        return (a % zs) * (ys * xs) + (b % ys) * xs + c % xs

    x_peers = [seq_of(z, y, x + d) for d in range(1, xs)]
    y_peers = [seq_of(z, y + d, x) for d in range(1, ys)]
    z_peers = [seq_of(z + d, y, x) for d in range(1, zs)]
    barrier = pltpu.get_barrier_semaphore()
    for d in range(1, 4):
        pl.semaphore_signal(barrier, inc=1, device_id={"chan": ch ^ d}, device_id_type=MESH)
    for p in x_peers + y_peers + z_peers:
        pl.semaphore_signal(barrier, inc=1, device_id={"seq": p}, device_id_type=MESH)
    pl.semaphore_wait(barrier, 3 + xs + ys + zs - 3)
    for p in y_peers:
        pl.semaphore_signal(row_sem, inc=1, device_id={"seq": p}, device_id_type=MESH)

    def chan_copy(src, dst, ss, rs, to):
        return pltpu.make_async_remote_copy(
            src_ref=src, dst_ref=dst, send_sem=ss, recv_sem=rs, device_id={"chan": to}, device_id_type=MESH
        )

    def factor_copy(which, n, ss, rs, owner, to, src=None):
        place = fac.at[which, n, rows(owner * quarter, quarter), :]
        return chan_copy(place if src is None else src.at[n], place, ss.at[which, n], rs.at[which, n], to)

    def to_sib(which, src):
        return [factor_copy(which, n, sib_send, sib_recv, ch, sib, src) for n in range(blocks)]

    def to_par(which, src):
        return [factor_copy(which, n, par_send, par_recv, ch, par, src) for n in range(blocks)]

    def passed_on(which):
        return [factor_copy(which, n, fwd_send, fwd_recv, par, sib) for n in range(blocks)]

    r_par, r_sib, r_fwd = to_par(RIGHT, r_hbm), to_sib(RIGHT, r_hbm), passed_on(RIGHT)
    l_par, l_sib, l_fwd = to_par(LEFT, l_hbm), to_sib(LEFT, l_hbm), passed_on(LEFT)
    for c in r_par + r_sib:
        c.start()

    def scatter_rows(local, count, base=0):
        for d in range(4):
            spread[pl.ds(base * piece + 4 * local + d, count, stride=piece), :] = part[pl.ds(d, count, stride=4), :]

    def send_piece(which, p):
        pltpu.make_async_remote_copy(
            src_ref=out_s.at[which, rows(p * piece, piece), :],
            dst_ref=out_r.at[which, rows(seq * piece, piece), :],
            send_sem=a2a_send.at[which],
            recv_sem=a2a_recv.at[which],
            device_id={"seq": p},
            device_id_type=MESH,
        ).start()

    def keep_own(which):
        here = rows(seq * piece, piece)
        out_r[which, here, :] = out_s[which, here, :]

    def send_all(which):
        def step(t, carry):
            u = (t * 37) % n_seq
            send_piece(which, seq_of(z + u // (ys * xs), y + (u // xs) % ys, x + u % xs))
            return carry

        lax.fori_loop(1, n_seq, step, 0)
        keep_own(which)

    def send_quarter(which, q):
        def step(t, carry):
            u = (t * 13) % dests
            p = q * dests + (seq + u) % dests

            @pl.when(p != seq)
            def _():
                send_piece(which, p)

            return carry

        lax.fori_loop(0, dests, step, 0)

    def wait_bytes(ref, sem):
        pltpu.make_async_copy(ref, ref, sem).wait()

    def wait_pieces(which, sem):
        wait_bytes(out_s.at[which, pl.ds(0, (n_seq - 1) * piece), :], sem.at[which])

    loads[0].wait()
    loads[1].wait()
    for n in range(blocks):
        block = pl.ds(n * order, order)
        part[...] = yv[block, :].astype(F32) * gv[block, :].astype(F32)
        scatter_rows(n, n_seq)
    out_s[BACK] = spread[...].astype(BF16)
    pl.semaphore_wait(row_sem, ys - 1)
    for p in z_peers:
        pl.semaphore_signal(plane_sem, inc=1, device_id={"seq": p}, device_id_type=MESH)
    loads[2].wait()
    loads[3].wait()

    def upper_quarter(q):
        for n in range(blocks):
            part[pl.ds(0, quarter), :] = dot(fac[RIGHT, n, rows(q * quarter, quarter), :], xv[pl.ds(n * order, order), :])
            scatter_rows(n, dests)
        size = dests * piece
        out_s[UPPER, rows(q * size, size), :] = spread[pl.ds(0, size), :].astype(BF16)

    upper_quarter(ch)
    pl.semaphore_wait(plane_sem, zs - 1)
    send_all(BACK)
    send_quarter(UPPER, ch)
    for c in r_sib:
        c.wait_recv()
    upper_quarter(sib)
    send_quarter(UPPER, sib)
    for c, f in zip(r_par, r_fwd):
        c.wait_recv()
        f.start()
    for c in l_par + l_sib:
        c.start()
    upper_quarter(par)
    send_quarter(UPPER, par)
    for f in r_fwd:
        f.wait_recv()
    upper_quarter(ch ^ 3)
    send_quarter(UPPER, ch ^ 3)
    keep_own(UPPER)

    for c, f in zip(l_par, l_fwd):
        c.wait_recv()
        f.start()
    loads[4].wait()
    wait_pieces(BACK, a2a_recv)
    flat[...] = out_r[BACK].astype(F32)
    for c in l_sib + l_fwd:
        c.wait_recv()
    for n in range(blocks):
        column = flat[pl.ds(n, order, stride=4), :]
        bk[n] = column.astype(BF16)
        part[...] = dot(column.T.astype(BF16), fac[LEFT, n]).T
        scatter_rows(n, n_seq)
    out_s[LOWER] = spread[...].astype(BF16)
    send_all(LOWER)

    wait_pieces(UPPER, a2a_recv)
    flat[...] = out_r[UPPER].astype(F32)
    for n in range(blocks):
        uk[n] = flat[pl.ds(n, order, stride=4), :].astype(BF16)
        part[...] = dot(fac[LEFT, n], uk[n])
        scatter_rows(n, n_seq)
    out_s[MIXED] = spread[...].astype(BF16)
    send_all(MIXED)

    def near_copy(which, n):
        return chan_copy(near_s.at[which, n], near_r.at[which, n], near_ss.at[which, n], near_rs.at[which, n], sib)

    def home_copy(which, n):
        return chan_copy(home_s.at[which, n], home_r.at[which, n], home_ss.at[which, n], home_rs.at[which, n], sib)

    def far_copy(which, n):
        return chan_copy(far_s.at[which, n], far_r.at[which, n], far_ss.at[which, n], far_rs.at[which, n], par)

    def grad_terms(which, a, b):
        def term(n, q):
            return dot(a(n, rows(q * quarter, quarter)), b(n), ((1,), (1,)))

        for n in range(blocks):
            near_s[which, n] = term(n, ch ^ 3).astype(BF16)
            near_copy(which, n).start()
        for n in range(blocks):
            far_f[n] = term(n, par)
        for n in range(blocks):
            near_copy(which, n).wait_recv()
            far_s[which, n] = (far_f[n] + near_r[which, n].astype(F32)).astype(BF16)
            far_copy(which, n).start()
        for n in range(blocks):
            home_s[which, n] = term(n, sib).astype(BF16)
            home_copy(which, n).start()
        for n in range(blocks):
            home_f[which, n] = term(n, ch)

    def grad_total(which, dst):
        for n in range(blocks):
            home_copy(which, n).wait_recv()
            far_copy(which, n).wait_recv()
            total = home_f[which, n] + home_r[which, n].astype(F32) + far_r[which, n].astype(F32)
            grad[which, n] = total.astype(BF16)
        copy = pltpu.make_async_copy(grad.at[which], dst, out_sem.at[which])
        copy.start()
        return copy

    grad_terms(LEFT, lambda n, r: bk[n, r, :], lambda n: uk[n])

    wait_pieces(LOWER, a2a_recv)
    flat[...] = out_r[LOWER].astype(F32)
    for n in range(blocks):
        lk[n] = flat[pl.ds(n, order, stride=4), :].astype(BF16)
    grad_terms(RIGHT, lambda n, r: lk[n, r, :], lambda n: xv[pl.ds(n * order, order), :])
    for n in range(blocks):
        column = flat[pl.ds(n, order, stride=4), :]
        ig[pl.ds(n * order, order), :] = dot(column.T.astype(BF16), fac[RIGHT, n]).T.astype(BF16)
    ig_out = pltpu.make_async_copy(ig, ig_hbm, out_sem.at[2])
    ig_out.start()

    wait_pieces(MIXED, a2a_recv)
    flat[...] = out_r[MIXED].astype(F32)
    for n in range(blocks):
        block = pl.ds(n * order, order)
        gg[block, :] = (yv[block, :].astype(F32) * flat[pl.ds(n, order, stride=4), :]).astype(BF16)
    gg_out = pltpu.make_async_copy(gg, gg_hbm, out_sem.at[3])
    gg_out.start()

    lg_out = grad_total(LEFT, lg_hbm)
    rg_out = grad_total(RIGHT, rg_hbm)
    for which in range(4):
        wait_pieces(which, a2a_send)
    for c in r_par + r_sib + r_fwd + l_par + l_sib + l_fwd:
        c.wait_send()
    for which in range(2):
        for n in range(blocks):
            near_copy(which, n).wait_send()
            home_copy(which, n).wait_send()
            far_copy(which, n).wait_send()
    for c in (ig_out, gg_out, lg_out, rg_out):
        c.wait()


def shards(n_seq, inputs, gate, cotangent, right_factor, left_factor):
    tokens, width = inputs.shape
    blocks, quarter, order = right_factor.shape
    piece = 4 * blocks
    data = (tokens, width)
    exchange = (4, n_seq * piece, width)
    terms = (2, blocks, quarter, order)
    dma = pltpu.SemaphoreType.DMA
    per_block = dma((2, blocks))
    scratch = (
        [pltpu.VMEM(data, BF16)] * 3
        + [pltpu.VMEM((2, blocks, order, order), BF16)]
        + [pltpu.VMEM(exchange, BF16)] * 2
        + [pltpu.VMEM((order, width), F32), pltpu.VMEM(exchange[1:], F32), pltpu.VMEM(exchange[1:], F32)]
        + [pltpu.VMEM((blocks, order, width), BF16)] * 3
        + [pltpu.VMEM(data, BF16)] * 2
        + [pltpu.VMEM(terms, BF16)] * 6
        + [pltpu.VMEM(terms[1:], F32), pltpu.VMEM(terms, F32), pltpu.VMEM(terms, BF16)]
        + [dma((LOADS,)), dma((4,)), dma((4,))]
        + [per_block] * 6
        + [per_block] * 6
        + [dma((4,)), pltpu.SemaphoreType.REGULAR, pltpu.SemaphoreType.REGULAR]
    )
    anywhere = pl.BlockSpec(memory_space=pl.ANY)
    flops = 12 * blocks * order * order * width
    return pl.pallas_call(
        functools.partial(kernel, n_seq),
        out_shape=(
            jax.ShapeDtypeStruct(data, BF16),
            jax.ShapeDtypeStruct(data, BF16),
            jax.ShapeDtypeStruct(right_factor.shape, BF16),
            jax.ShapeDtypeStruct(left_factor.shape, BF16),
        ),
        in_specs=[anywhere] * 5,
        out_specs=(anywhere,) * 4,
        scratch_shapes=scratch,
        compiler_params=pltpu.CompilerParams(
            collective_id=0, has_side_effects=True, vmem_limit_bytes=48 * 2**20
        ),
        cost_estimate=pl.CostEstimate(flops=flops, bytes_accessed=9 * 2**19, transcendentals=0),
        name="monarch",
    )(inputs, gate, cotangent, right_factor, left_factor)


def solution(mesh):
    rows = P("seq", "chan")
    factor = P("seq", "chan", None)
    return jax.shard_map(
        functools.partial(shards, mesh.shape["seq"]),
        mesh=mesh,
        in_specs=(rows, rows, rows, factor, factor),
        out_specs=(rows, rows, factor, factor),
        check_vma=False,
    )
```

```python
import functools

import jax
import jax.numpy as jnp
from jax import lax
from jax.experimental import pallas as pl
from jax.experimental.pallas import tpu as pltpu
from jax.sharding import PartitionSpec as P

MESH = pl.DeviceIdType.MESH
BF16 = jnp.bfloat16
F32 = jnp.float32
LOADS = 5
UPPER, MIXED, BACK, LOWER = range(4)
RIGHT, LEFT = range(2)


def torus(n_seq):
    return {128: (8, 4, 4), 8: (2, 2, 2)}[n_seq]


def dot(a, b, dims=((1,), (0,))):
    return lax.dot_general(a, b, (dims, ((), ())), preferred_element_type=F32)


def kernel(
    n_seq,
    x_hbm, g_hbm, y_hbm, r_hbm, l_hbm,
    ig_hbm, gg_hbm, rg_hbm, lg_hbm,
    xv, gv, yv, fac, out_s, out_r, part, spread, flat,
    bk, uk, lk,
    ig, gg, near_s, near_r, home_s, home_r, far_s, far_r, far_f, home_f, grad,
    load_sem, a2a_send, a2a_recv, sib_send, sib_recv, par_send, par_recv, fwd_send, fwd_recv,
    near_ss, near_rs, home_ss, home_rs, far_ss, far_rs, out_sem, row_sem, plane_sem,
):
    zs, ys, xs = torus(n_seq)
    blocks, order, width = fac.shape[1], fac.shape[2], xv.shape[1]
    quarter = order // 4
    dests = n_seq // 4
    piece = 4 * blocks
    seq, ch = lax.axis_index("seq"), lax.axis_index("chan")
    z, y, x = seq // (ys * xs), (seq // xs) & (ys - 1), seq & (xs - 1)
    sib, par = ch ^ 1, ch ^ 2

    def rows(start, size):
        return pl.ds(pl.multiple_of(start, size), size)

    mine = rows(ch * quarter, quarter)
    loads = [
        pltpu.make_async_copy(src, dst, load_sem.at[n])
        for n, (src, dst) in enumerate((
            (y_hbm, yv), (g_hbm, gv), (x_hbm, xv),
            (r_hbm, fac.at[RIGHT, :, mine, :]), (l_hbm, fac.at[LEFT, :, mine, :]),
        ))
    ]
    for load in loads:
        load.start()

    def seq_of(a, b, c):
        return (a & (zs - 1)) * (ys * xs) + (b & (ys - 1)) * xs + (c & (xs - 1))

    x_peers = [seq_of(z, y, x + d) for d in range(1, xs)]
    y_peers = [seq_of(z, y + d, x) for d in range(1, ys)]
    z_peers = [seq_of(z + d, y, x) for d in range(1, zs)]
    barrier = pltpu.get_barrier_semaphore()
    for d in range(1, 4):
        pl.semaphore_signal(barrier, inc=1, device_id={"chan": ch ^ d}, device_id_type=MESH)
    for p in x_peers + y_peers + z_peers:
        pl.semaphore_signal(barrier, inc=1, device_id={"seq": p}, device_id_type=MESH)
    pl.semaphore_wait(barrier, 3 + xs + ys + zs - 3)
    for p in y_peers:
        pl.semaphore_signal(row_sem, inc=1, device_id={"seq": p}, device_id_type=MESH)

    def chan_copy(src, dst, ss, rs, to):
        return pltpu.make_async_remote_copy(
            src_ref=src, dst_ref=dst, send_sem=ss, recv_sem=rs, device_id={"chan": to}, device_id_type=MESH
        )

    def factor_copy(which, n, ss, rs, owner, to, src=None):
        place = fac.at[which, n, rows(owner * quarter, quarter), :]
        return chan_copy(place if src is None else src.at[n], place, ss.at[which, n], rs.at[which, n], to)

    def to_sib(which, src):
        return [factor_copy(which, n, sib_send, sib_recv, ch, sib, src) for n in range(blocks)]

    def to_par(which, src):
        return [factor_copy(which, n, par_send, par_recv, ch, par, src) for n in range(blocks)]

    def passed_on(which):
        return [factor_copy(which, n, fwd_send, fwd_recv, par, sib) for n in range(blocks)]

    r_par, r_sib, r_fwd = to_par(RIGHT, r_hbm), to_sib(RIGHT, r_hbm), passed_on(RIGHT)
    l_par, l_sib, l_fwd = to_par(LEFT, l_hbm), to_sib(LEFT, l_hbm), passed_on(LEFT)
    for c in r_par + r_sib:
        c.start()

    def scatter_rows(local, count, base=0):
        for d in range(4):
            spread[pl.ds(base * piece + 4 * local + d, count, stride=piece), :] = part[pl.ds(d, count, stride=4), :]

    def send_piece(which, p):
        pltpu.make_async_remote_copy(
            src_ref=out_s.at[which, rows(p * piece, piece), :],
            dst_ref=out_r.at[which, rows(seq * piece, piece), :],
            send_sem=a2a_send.at[which],
            recv_sem=a2a_recv.at[which],
            device_id={"seq": p},
            device_id_type=MESH,
        ).start()

    def keep_own(which):
        here = rows(seq * piece, piece)
        out_r[which, here, :] = out_s[which, here, :]

    def send_all(which):
        def step(t, carry):
            u = (t * 37) & (n_seq - 1)
            send_piece(which, seq_of(z + u // (ys * xs), y + u // xs, x + u))
            return carry

        lax.fori_loop(1, n_seq, step, 0)
        keep_own(which)

    def send_quarter(which, q):
        def step(t, carry):
            u = (t * 13) & (dests - 1)
            p = q * dests + ((seq + u) & (dests - 1))

            @pl.when(p != seq)
            def _():
                send_piece(which, p)

            return carry

        lax.fori_loop(0, dests, step, 0)

    def wait_bytes(ref, sem):
        pltpu.make_async_copy(ref, ref, sem).wait()

    def wait_pieces(which, sem):
        wait_bytes(out_s.at[which, pl.ds(0, (n_seq - 1) * piece), :], sem.at[which])

    loads[0].wait()
    loads[1].wait()
    for n in range(blocks):
        block = pl.ds(n * order, order)
        part[...] = yv[block, :].astype(F32) * gv[block, :].astype(F32)
        scatter_rows(n, n_seq)
    out_s[BACK] = spread[...].astype(BF16)
    pl.semaphore_wait(row_sem, ys - 1)
    for p in z_peers:
        pl.semaphore_signal(plane_sem, inc=1, device_id={"seq": p}, device_id_type=MESH)
    loads[2].wait()
    loads[3].wait()

    def upper_quarter(q):
        for n in range(blocks):
            part[pl.ds(0, quarter), :] = dot(fac[RIGHT, n, rows(q * quarter, quarter), :], xv[pl.ds(n * order, order), :])
            scatter_rows(n, dests)
        size = dests * piece
        out_s[UPPER, rows(q * size, size), :] = spread[pl.ds(0, size), :].astype(BF16)

    upper_quarter(ch)
    pl.semaphore_wait(plane_sem, zs - 1)
    send_all(BACK)
    send_quarter(UPPER, ch)
    for c in r_sib:
        c.wait_recv()
    upper_quarter(sib)
    send_quarter(UPPER, sib)
    for c, f in zip(r_par, r_fwd):
        c.wait_recv()
        f.start()
    for c in l_par + l_sib:
        c.start()
    upper_quarter(par)
    send_quarter(UPPER, par)
    for f in r_fwd:
        f.wait_recv()
    upper_quarter(ch ^ 3)
    send_quarter(UPPER, ch ^ 3)
    keep_own(UPPER)

    for c, f in zip(l_par, l_fwd):
        c.wait_recv()
        f.start()
    loads[4].wait()
    wait_pieces(BACK, a2a_recv)
    flat[...] = out_r[BACK].astype(F32)
    for c in l_sib + l_fwd:
        c.wait_recv()
    for n in range(blocks):
        column = flat[pl.ds(n, order, stride=4), :]
        bk[n] = column.astype(BF16)
        part[...] = dot(column.T.astype(BF16), fac[LEFT, n]).T
        scatter_rows(n, n_seq)
    out_s[LOWER] = spread[...].astype(BF16)
    send_all(LOWER)

    wait_pieces(UPPER, a2a_recv)
    flat[...] = out_r[UPPER].astype(F32)
    for n in range(blocks):
        uk[n] = flat[pl.ds(n, order, stride=4), :].astype(BF16)
        part[...] = dot(fac[LEFT, n], uk[n])
        scatter_rows(n, n_seq)
    out_s[MIXED] = spread[...].astype(BF16)
    send_all(MIXED)

    def near_copy(which, n):
        return chan_copy(near_s.at[which, n], near_r.at[which, n], near_ss.at[which, n], near_rs.at[which, n], sib)

    def home_copy(which, n):
        return chan_copy(home_s.at[which, n], home_r.at[which, n], home_ss.at[which, n], home_rs.at[which, n], sib)

    def far_copy(which, n):
        return chan_copy(far_s.at[which, n], far_r.at[which, n], far_ss.at[which, n], far_rs.at[which, n], par)

    def grad_terms(which, a, b):
        def term(n, q):
            return dot(a(n, rows(q * quarter, quarter)), b(n), ((1,), (1,)))

        for n in range(blocks):
            near_s[which, n] = term(n, ch ^ 3).astype(BF16)
            near_copy(which, n).start()
        for n in range(blocks):
            far_f[n] = term(n, par)
        for n in range(blocks):
            near_copy(which, n).wait_recv()
            far_s[which, n] = (far_f[n] + near_r[which, n].astype(F32)).astype(BF16)
            far_copy(which, n).start()
        for n in range(blocks):
            home_s[which, n] = term(n, sib).astype(BF16)
            home_copy(which, n).start()
        for n in range(blocks):
            home_f[which, n] = term(n, ch)

    def grad_total(which, dst):
        for n in range(blocks):
            home_copy(which, n).wait_recv()
            far_copy(which, n).wait_recv()
            total = home_f[which, n] + home_r[which, n].astype(F32) + far_r[which, n].astype(F32)
            grad[which, n] = total.astype(BF16)
        copy = pltpu.make_async_copy(grad.at[which], dst, out_sem.at[which])
        copy.start()
        return copy

    grad_terms(LEFT, lambda n, r: bk[n, r, :], lambda n: uk[n])

    wait_pieces(LOWER, a2a_recv)
    flat[...] = out_r[LOWER].astype(F32)
    for n in range(blocks):
        lk[n] = flat[pl.ds(n, order, stride=4), :].astype(BF16)
    grad_terms(RIGHT, lambda n, r: lk[n, r, :], lambda n: xv[pl.ds(n * order, order), :])
    for n in range(blocks):
        column = flat[pl.ds(n, order, stride=4), :]
        ig[pl.ds(n * order, order), :] = dot(column.T.astype(BF16), fac[RIGHT, n]).T.astype(BF16)
    ig_out = pltpu.make_async_copy(ig, ig_hbm, out_sem.at[2])
    ig_out.start()

    wait_pieces(MIXED, a2a_recv)
    flat[...] = out_r[MIXED].astype(F32)
    for n in range(blocks):
        block = pl.ds(n * order, order)
        gg[block, :] = (yv[block, :].astype(F32) * flat[pl.ds(n, order, stride=4), :]).astype(BF16)
    gg_out = pltpu.make_async_copy(gg, gg_hbm, out_sem.at[3])
    gg_out.start()

    lg_out = grad_total(LEFT, lg_hbm)
    rg_out = grad_total(RIGHT, rg_hbm)
    for which in range(4):
        wait_pieces(which, a2a_send)
    for c in r_par + r_sib + r_fwd + l_par + l_sib + l_fwd:
        c.wait_send()
    for which in range(2):
        for n in range(blocks):
            near_copy(which, n).wait_send()
            home_copy(which, n).wait_send()
            far_copy(which, n).wait_send()
    for c in (ig_out, gg_out, lg_out, rg_out):
        c.wait()


def hand_over(*refs):
    sem = refs[-1]
    copies = [pltpu.make_async_copy(refs[n], refs[4 + n], sem.at[n]) for n in range(4)]
    for c in copies:
        c.start()
    for c in copies:
        c.wait()


def shards(n_seq, inputs, gate, cotangent, right_factor, left_factor):
    tokens, width = inputs.shape
    blocks, quarter, order = right_factor.shape
    piece = 4 * blocks
    data = (tokens, width)
    exchange = (4, n_seq * piece, width)
    terms = (2, blocks, quarter, order)
    dma = pltpu.SemaphoreType.DMA
    per_block = dma((2, blocks))
    scratch = (
        [pltpu.VMEM(data, BF16)] * 3
        + [pltpu.VMEM((2, blocks, order, order), BF16)]
        + [pltpu.VMEM(exchange, BF16)] * 2
        + [pltpu.VMEM((order, width), F32), pltpu.VMEM(exchange[1:], F32), pltpu.VMEM(exchange[1:], F32)]
        + [pltpu.VMEM((blocks, order, width), BF16)] * 3
        + [pltpu.VMEM(data, BF16)] * 2
        + [pltpu.VMEM(terms, BF16)] * 6
        + [pltpu.VMEM(terms[1:], F32), pltpu.VMEM(terms, F32), pltpu.VMEM(terms, BF16)]
        + [dma((LOADS,)), dma((4,)), dma((4,))]
        + [per_block] * 6
        + [per_block] * 6
        + [dma((4,)), pltpu.SemaphoreType.REGULAR, pltpu.SemaphoreType.REGULAR]
    )
    in_hbm = pl.BlockSpec(memory_space=pltpu.HBM)
    flops = 12 * blocks * order * order * width
    results = pl.pallas_call(
        functools.partial(kernel, n_seq),
        out_shape=(
            jax.ShapeDtypeStruct(data, BF16),
            jax.ShapeDtypeStruct(data, BF16),
            jax.ShapeDtypeStruct(right_factor.shape, BF16),
            jax.ShapeDtypeStruct(left_factor.shape, BF16),
        ),
        in_specs=[in_hbm] * 5,
        out_specs=(in_hbm,) * 4,
        scratch_shapes=scratch,
        compiler_params=pltpu.CompilerParams(
            collective_id=0, has_side_effects=True, vmem_limit_bytes=48 * 2**20
        ),
        cost_estimate=pl.CostEstimate(flops=flops, bytes_accessed=9 * 2**19, transcendentals=0),
        name="monarch",
    )(*(pltpu.with_memory_space_constraint(a, pltpu.HBM) for a in (inputs, gate, cotangent, right_factor, left_factor)))
    return pl.pallas_call(
        hand_over,
        out_shape=tuple(jax.ShapeDtypeStruct(r.shape, r.dtype) for r in results),
        in_specs=[in_hbm] * 4,
        out_specs=(in_hbm,) * 4,
        scratch_shapes=[dma((4,))],
        name="hand_over",
    )(*results)


def solution(mesh):
    rows = P("seq", "chan")
    factor = P("seq", "chan", None)
    return jax.shard_map(
        functools.partial(shards, mesh.shape["seq"]),
        mesh=mesh,
        in_specs=(rows, rows, rows, factor, factor),
        out_specs=(rows, rows, factor, factor),
        check_vma=False,
    )
```

```python
import functools

import jax
import jax.numpy as jnp
from jax import lax
from jax.experimental import pallas as pl
from jax.experimental.pallas import tpu as pltpu
from jax.sharding import PartitionSpec as P

MESH = pl.DeviceIdType.MESH
BF16 = jnp.bfloat16
F32 = jnp.float32
UPPER, MIXED, BACK, LOWER = range(4)
RIGHT, LEFT = range(2)
OWN, SIB = range(2)


def torus(n_seq):
    return {128: (8, 4, 4), 8: (2, 2, 2)}[n_seq]


def dot(a, b, dims=((1,), (0,))):
    return lax.dot_general(a, b, (dims, ((), ())), preferred_element_type=F32)


def kernel(
    n_seq,
    x_hbm, g_hbm, y_hbm, r_hbm, l_hbm,
    ig_hbm, gg_hbm, rg_hbm, lg_hbm,
    xv, gv, yv, gated, right, left, out_s, out_r, sib_r, part, spread, flat,
    bk, uk, lk, ig, gg, far_s, far_r, far_l, home_f, grad,
    load_sem, a2a_send, a2a_recv, share_send, share_recv, in_send, in_recv,
    sib_send, sib_recv, par_send, par_recv, fwd_send, fwd_recv,
    far_ss, far_rs, out_sem, row_sem, plane_sem,
):
    zs, ys, xs = torus(n_seq)
    blocks, order, width = right.shape[0], right.shape[1], gv.shape[1]
    quarter = order // 4
    dests = n_seq // 4
    piece = 4 * blocks
    seq, ch = lax.axis_index("seq"), lax.axis_index("chan")
    z, y, x = seq // (ys * xs), (seq // xs) & (ys - 1), seq & (xs - 1)
    chip, core = ch // 2, ch & 1
    sib, par, twist = ch ^ 1, ch ^ 2, 2 * core + chip

    def rows(start, size):
        return pl.ds(pl.multiple_of(start, size), size)

    def lanes(r):
        return pl.ds(r * width, width)

    mine = rows(ch * quarter, quarter)
    loads = [
        pltpu.make_async_copy(src, dst, load_sem.at[n])
        for n, (src, dst) in enumerate((
            (y_hbm, yv), (g_hbm, gv), (r_hbm, right.at[:, mine, :]), (x_hbm, xv.at[:, lanes(OWN)]),
            (l_hbm.at[pl.ds(2 * chip, 2)], left.at[:, mine, :]),
        ))
    ]
    for load in loads:
        load.start()

    def seq_of(a, b, c):
        return (a & (zs - 1)) * (ys * xs) + (b & (ys - 1)) * xs + (c & (xs - 1))

    y_peers = [seq_of(z, y + d, x) for d in range(1, ys)]
    z_peers = [seq_of(z + d, y, x) for d in range(1, zs)]
    barrier = pltpu.get_barrier_semaphore()
    for d in range(1, 4):
        pl.semaphore_signal(barrier, inc=1, device_id={"chan": ch ^ d}, device_id_type=MESH)
    for p in y_peers + z_peers:
        pl.semaphore_signal(barrier, inc=1, device_id={"seq": p}, device_id_type=MESH)
    for d in range(1, xs):
        to = {"seq": seq_of(z, y, x + d), "chan": twist}
        pl.semaphore_signal(barrier, inc=1, device_id=to, device_id_type=MESH)
    pl.semaphore_wait(barrier, 3 + xs + ys + zs - 3)

    def chan_copy(src, dst, ss, rs, to):
        return pltpu.make_async_remote_copy(
            src_ref=src, dst_ref=dst, send_sem=ss, recv_sem=rs, device_id={"chan": to}, device_id_type=MESH
        )

    def right_copy(n, sems, owner, to, src=None):
        place = right.at[n, rows(owner * quarter, quarter), :]
        return chan_copy(place if src is None else src, place, sems[0].at[RIGHT, n], sems[1].at[RIGHT, n], to)

    def left_copy(n, sems, owner, to, src=None):
        place = left.at[n, rows(owner * quarter, quarter), :]
        return chan_copy(place if src is None else src, place, sems[0].at[LEFT, n], sems[1].at[LEFT, n], to)

    sib_sems, par_sems, fwd_sems = (sib_send, sib_recv), (par_send, par_recv), (fwd_send, fwd_recv)
    r_par = [right_copy(n, par_sems, ch, par, r_hbm.at[n]) for n in range(blocks)]
    r_sib = [right_copy(n, sib_sems, ch, sib, r_hbm.at[n]) for n in range(blocks)]
    r_fwd = [right_copy(n, fwd_sems, par, sib) for n in range(blocks)]
    l_par = [left_copy(n, par_sems, ch, par, l_hbm.at[2 * (1 - chip) + n]) for n in range(2)]
    l_sib = [left_copy(n, sib_sems, ch, sib, l_hbm.at[2 * chip + n]) for n in range(2)]
    l_fwd = [left_copy(n, fwd_sems, par, sib) for n in range(2)]
    x_sib = chan_copy(x_hbm, xv.at[:, lanes(SIB)], in_send.at[0], in_recv.at[0], sib)
    b_sib = chan_copy(gated.at[OWN], gated.at[SIB], in_send.at[1], in_recv.at[1], sib)
    for c in r_par + [x_sib] + r_sib:
        c.start()
    for p in y_peers:
        pl.semaphore_signal(row_sem, inc=1, device_id={"seq": p}, device_id_type=MESH)

    def to_piece(r, row, first, count):
        spread[pl.ds(row, count, stride=piece), :] = part[r, pl.ds(first, count, stride=4), :]

    def to_columns(r, local, count):
        for d in range(2):
            to_piece(r, 4 * local + 2 * d + r, 2 * core + d, count)

    def to_positions(r, d):
        for local in range(4):
            to_piece(r, 4 * (2 * d + r) + local, local, n_seq)

    def piece_copy(which, p):
        return pltpu.make_async_remote_copy(
            src_ref=out_s.at[which, rows(p * piece, piece), :],
            dst_ref=out_r.at[which, rows(seq * piece, piece), :],
            send_sem=a2a_send.at[which],
            recv_sem=a2a_recv.at[which],
            device_id={"seq": p, "chan": twist},
            device_id_type=MESH,
        )

    def send_own(which):
        @pl.when(chip == core)
        def _():
            here = rows(seq * piece, piece)
            out_r[which, here, :] = out_s[which, here, :]

        @pl.when(chip != core)
        def _():
            piece_copy(which, seq).start()

    def send_all(which):
        def step(t, carry):
            u = (t * 37) & (n_seq - 1)
            piece_copy(which, seq_of(z + u // (ys * xs), y + u // xs, x + u)).start()
            return carry

        lax.fori_loop(1, n_seq, step, 0)
        send_own(which)

    def send_quarter(which, q):
        def step(t, carry):
            u = (t * 13) & (dests - 1)
            p = q * dests + ((seq + u) & (dests - 1))

            @pl.when(p != seq)
            def _():
                piece_copy(which, p).start()

            return carry

        lax.fori_loop(0, dests, step, 0)

    def wait_pieces(which, sem):
        def wait_for(count):
            ref = out_s.at[which, pl.ds(0, count * piece), :]
            pltpu.make_async_copy(ref, ref, sem.at[which]).wait()

        pl.when(chip == core)(lambda: wait_for(n_seq - 1))
        pl.when(chip != core)(lambda: wait_for(n_seq))

    def share(which):
        return chan_copy(out_r.at[which], sib_r.at[which], share_send.at[which], share_recv.at[which], sib)

    def arrived(which):
        wait_pieces(which, a2a_recv)
        share(which).start()
        flat[OWN] = out_r[which].astype(F32)

    def shared(which):
        share(which).wait_recv()
        flat[SIB] = sib_r[which].astype(F32)

    loads[0].wait()
    loads[1].wait()
    for n in range(blocks):
        block = pl.ds(n * order, order)
        part[OWN] = yv[block, :].astype(F32) * gv[block, :].astype(F32)
        gated[OWN, block, :] = part[OWN].astype(BF16)
        to_columns(OWN, n, n_seq)
    b_sib.start()
    pl.semaphore_wait(row_sem, ys - 1)
    for p in z_peers:
        pl.semaphore_signal(plane_sem, inc=1, device_id={"seq": p}, device_id_type=MESH)
    b_sib.wait_recv()
    for n in range(blocks):
        part[SIB] = gated[SIB, pl.ds(n * order, order), :].astype(F32)
        to_columns(SIB, n, n_seq)
    out_s[BACK] = spread[...].astype(BF16)
    pl.semaphore_wait(plane_sem, zs - 1)
    send_all(BACK)

    def upper_quarter(q):
        here = pl.ds(0, quarter)
        for n in range(blocks):
            terms = dot(right[n, rows(q * quarter, quarter), :], xv[pl.ds(n * order, order), :])
            for r in range(2):
                part[r, here, :] = terms[:, r * width:(r + 1) * width]
                to_columns(r, n, dests)
        size = dests * piece
        out_s[UPPER, rows(q * size, size), :] = spread[pl.ds(0, size), :].astype(BF16)
        send_quarter(UPPER, q)

    loads[2].wait()
    loads[3].wait()
    x_sib.wait_recv()
    upper_quarter(ch)
    for c in r_sib:
        c.wait_recv()
    upper_quarter(sib)
    for c, f in zip(r_par, r_fwd):
        c.wait_recv()
        f.start()
    for c in l_par + l_sib:
        c.start()
    upper_quarter(par)
    for f in r_fwd:
        f.wait_recv()
    upper_quarter(ch ^ 3)
    send_own(UPPER)

    for c, f in zip(l_par, l_fwd):
        c.wait_recv()
        f.start()
    loads[4].wait()
    arrived(BACK)
    for c in l_sib + l_fwd:
        c.wait_recv()
    for d in range(2):
        column = [flat[OWN, pl.ds(2 * d + r, order, stride=4), :] for r in range(2)]
        for r in range(2):
            bk[d, :, lanes(r)] = column[r].astype(BF16)
        turned = jnp.concatenate([column[r].T for r in range(2)], axis=0).astype(BF16)
        terms = dot(turned, left[d])
        for r in range(2):
            part[r] = terms[r * width:(r + 1) * width].T
            to_positions(r, d)
    out_s[LOWER] = spread[...].astype(BF16)
    send_all(LOWER)

    arrived(UPPER)
    for d in range(2):
        for r in range(2):
            uk[d, :, lanes(r)] = flat[OWN, pl.ds(2 * d + r, order, stride=4), :].astype(BF16)
        terms = dot(left[d], uk[d, :, pl.ds(0, 2 * width)])
        for r in range(2):
            part[r] = terms[:, r * width:(r + 1) * width]
            to_positions(r, d)
    out_s[MIXED] = spread[...].astype(BF16)
    send_all(MIXED)

    for which, dst in ((BACK, bk), (UPPER, uk)):
        shared(which)
        for d in range(2):
            for r in range(2):
                dst[d, :, lanes(2 + r)] = flat[SIB, pl.ds(2 * d + r, order, stride=4), :].astype(BF16)

    def left_far(d):
        place = grad.at[LEFT, 2 * chip + d]
        return chan_copy(far_l.at[d], place, far_ss.at[LEFT, d], far_rs.at[LEFT, d], par)

    for d in range(2):
        far_l[d] = dot(bk[d, rows(par * quarter, quarter), :], uk[d], ((1,), (1,))).astype(BF16)
        left_far(d).start()
    for d in range(2):
        grad[LEFT, 2 * chip + d] = dot(bk[d, rows(ch * quarter, quarter), :], uk[d], ((1,), (1,))).astype(BF16)

    def right_far(n):
        return chan_copy(far_s.at[n], far_r.at[n], far_ss.at[RIGHT, n], far_rs.at[RIGHT, n], par)

    def right_terms(n, q):
        return dot(lk[n, rows(q * quarter, quarter), :], xv[pl.ds(n * order, order), :], ((1,), (1,)))

    arrived(LOWER)
    shared(LOWER)
    for n in range(blocks):
        for held in (OWN, SIB):
            for d in range(2):
                for r in range(2):
                    part[r, pl.ds(2 * (core ^ held) + d, n_seq, stride=4), :] = (
                        flat[held, pl.ds(4 * (2 * d + (r ^ held)) + n, n_seq, stride=piece), :]
                    )
        for r in range(2):
            lk[n, :, lanes(r)] = part[r].astype(BF16)
        far_s[n] = right_terms(n, par).astype(BF16)
        right_far(n).start()
    for n in range(blocks):
        turned = lk[n, :, lanes(OWN)].astype(F32).T.astype(BF16)
        ig[pl.ds(n * order, order), :] = dot(turned, right[n]).T.astype(BF16)
    ig_out = pltpu.make_async_copy(ig, ig_hbm, out_sem.at[2])
    ig_out.start()
    for n in range(blocks):
        home_f[n] = right_terms(n, ch)

    arrived(MIXED)
    shared(MIXED)
    for n in range(blocks):
        block = pl.ds(n * order, order)
        for held in (OWN, SIB):
            for d in range(2):
                part[0, pl.ds(2 * (core ^ held) + d, n_seq, stride=4), :] = (
                    flat[held, pl.ds(4 * (2 * d + held) + n, n_seq, stride=piece), :]
                )
        gg[block, :] = (yv[block, :].astype(F32) * part[0]).astype(BF16)
    gg_out = pltpu.make_async_copy(gg, gg_hbm, out_sem.at[3])
    gg_out.start()

    for d in range(2):
        left_far(d).wait_recv()
    lg_out = pltpu.make_async_copy(grad.at[LEFT], lg_hbm, out_sem.at[LEFT])
    lg_out.start()
    for n in range(blocks):
        right_far(n).wait_recv()
        grad[RIGHT, n] = (home_f[n] + far_r[n].astype(F32)).astype(BF16)
    rg_out = pltpu.make_async_copy(grad.at[RIGHT], rg_hbm, out_sem.at[RIGHT])
    rg_out.start()

    for which in range(4):
        wait_pieces(which, a2a_send)
        share(which).wait_send()
    for c in r_par + r_sib + r_fwd + l_par + l_sib + l_fwd + [x_sib, b_sib]:
        c.wait_send()
    for d in range(2):
        left_far(d).wait_send()
    for n in range(blocks):
        right_far(n).wait_send()
    for c in (ig_out, gg_out, lg_out, rg_out):
        c.wait()


def hand_over(*refs):
    sem = refs[-1]
    copies = [pltpu.make_async_copy(refs[n], refs[4 + n], sem.at[n]) for n in range(4)]
    for c in copies:
        c.start()
    for c in copies:
        c.wait()


def shards(n_seq, inputs, gate, cotangent, right_factor, left_factor):
    tokens, width = inputs.shape
    blocks, quarter, order = right_factor.shape
    piece = 4 * blocks
    data = (tokens, width)
    pieces = (n_seq * piece, width)
    terms = (blocks, quarter, order)
    dma = pltpu.SemaphoreType.DMA
    per_block = dma((2, blocks))
    scratch = (
        [pltpu.VMEM((tokens, 2 * width), BF16)]
        + [pltpu.VMEM(data, BF16)] * 2
        + [pltpu.VMEM((2,) + data, BF16)]
        + [pltpu.VMEM((blocks, order, order), BF16), pltpu.VMEM((2, order, order), BF16)]
        + [pltpu.VMEM((4,) + pieces, BF16)] * 3
        + [pltpu.VMEM((2, order, width), F32), pltpu.VMEM(pieces, F32), pltpu.VMEM((2,) + pieces, F32)]
        + [pltpu.VMEM((2, order, 4 * width), BF16)] * 2
        + [pltpu.VMEM((blocks, order, 2 * width), BF16)]
        + [pltpu.VMEM(data, BF16)] * 2
        + [pltpu.VMEM(terms, BF16)] * 2
        + [pltpu.VMEM((2, quarter, order), BF16), pltpu.VMEM(terms, F32), pltpu.VMEM((2,) + terms, BF16)]
        + [dma((5,))]
        + [dma((4,))] * 4
        + [dma((2,))] * 2
        + [per_block] * 6
        + [per_block] * 2
        + [dma((4,)), pltpu.SemaphoreType.REGULAR, pltpu.SemaphoreType.REGULAR]
    )
    in_hbm = pl.BlockSpec(memory_space=pltpu.HBM)

    given = (inputs, gate, cotangent, right_factor, left_factor)
    results = pl.pallas_call(
        functools.partial(kernel, n_seq),
        out_shape=(
            jax.ShapeDtypeStruct(data, BF16),
            jax.ShapeDtypeStruct(data, BF16),
            jax.ShapeDtypeStruct(right_factor.shape, BF16),
            jax.ShapeDtypeStruct(left_factor.shape, BF16),
        ),
        in_specs=[in_hbm] * 5,
        out_specs=(in_hbm,) * 4,
        scratch_shapes=scratch,
        compiler_params=pltpu.CompilerParams(
            collective_id=0, has_side_effects=True, vmem_limit_bytes=48 * 2**20
        ),
        cost_estimate=pl.CostEstimate(
            flops=12 * blocks * order * order * width, bytes_accessed=9 * 2**19, transcendentals=0
        ),
        name="monarch",
    )(*(pltpu.with_memory_space_constraint(a, pltpu.HBM) for a in given))
    return pl.pallas_call(
        hand_over,
        out_shape=tuple(jax.ShapeDtypeStruct(r.shape, r.dtype) for r in results),
        in_specs=[pl.BlockSpec(memory_space=pltpu.VMEM)] * 4,
        out_specs=(in_hbm,) * 4,
        scratch_shapes=[dma((4,))],
        name="hand_over",
    )(*results)


def solution(mesh):
    rows = P("seq", "chan")
    factor = P("seq", "chan", None)
    return jax.shard_map(
        functools.partial(shards, mesh.shape["seq"]),
        mesh=mesh,
        in_specs=(rows, rows, rows, factor, factor),
        out_specs=(rows, rows, factor, factor),
        check_vma=False,
    )
```

```python
import functools

import jax
import jax.numpy as jnp
from jax import lax
from jax.experimental import pallas as pl
from jax.experimental.pallas import tpu as pltpu
from jax.sharding import PartitionSpec as P

MESH = pl.DeviceIdType.MESH
BF16 = jnp.bfloat16
F32 = jnp.float32
UPPER, MIXED, BACK, LOWER = range(4)
RIGHT, LEFT = range(2)
OWN, SIB = range(2)


def torus(n_seq):
    return {128: (8, 4, 4), 8: (2, 2, 2)}[n_seq]


def dot(a, b, dims=((1,), (0,))):
    return lax.dot_general(a, b, (dims, ((), ())), preferred_element_type=F32)


def kernel(
    n_seq,
    x_hbm, g_hbm, y_hbm, r_hbm, l_hbm,
    ig_hbm, gg_hbm, rg_hbm, lg_hbm,
    xv, gv, yv, gated, right, left, out_s, out_r, sib_r, part, spread, flat,
    bk, uk, lk, ig, gg, far_s, far_r, far_l, home_f, grad,
    load_sem, a2a_send, a2a_recv, share_send, share_recv, in_send, in_recv,
    sib_send, sib_recv, par_send, par_recv, fwd_send, fwd_recv,
    far_ss, far_rs, out_sem, row_sem, plane_sem,
):
    zs, ys, xs = torus(n_seq)
    blocks, order, width = right.shape[0], right.shape[1], gv.shape[1]
    quarter = order // 4
    dests = n_seq // 4
    piece = 4 * blocks
    seq, ch = lax.axis_index("seq"), lax.axis_index("chan")
    z, y, x = seq // (ys * xs), (seq // xs) & (ys - 1), seq & (xs - 1)
    chip, core = ch // 2, ch & 1
    sib, par, twist = ch ^ 1, ch ^ 2, 2 * core + chip

    def rows(start, size):
        return pl.ds(pl.multiple_of(start, size), size)

    def lanes(r):
        return pl.ds(r * width, width)

    mine = rows(ch * quarter, quarter)
    loads = [
        pltpu.make_async_copy(src, dst, load_sem.at[n])
        for n, (src, dst) in enumerate((
            (y_hbm, yv), (g_hbm, gv), (r_hbm, right.at[:, mine, :]), (x_hbm, xv.at[:, lanes(OWN)]),
            (l_hbm.at[pl.ds(2 * chip, 2)], left.at[:, mine, :]),
        ))
    ]
    for load in loads:
        load.start()

    def seq_of(a, b, c):
        return (a & (zs - 1)) * (ys * xs) + (b & (ys - 1)) * xs + (c & (xs - 1))

    y_peers = [seq_of(z, y + d, x) for d in range(1, ys)]
    z_peers = [seq_of(z + d, y, x) for d in range(1, zs)]
    barrier = pltpu.get_barrier_semaphore()
    for d in range(1, 4):
        pl.semaphore_signal(barrier, inc=1, device_id={"chan": ch ^ d}, device_id_type=MESH)
    for p in y_peers + z_peers:
        pl.semaphore_signal(barrier, inc=1, device_id={"seq": p}, device_id_type=MESH)
    for d in range(1, xs):
        to = {"seq": seq_of(z, y, x + d), "chan": twist}
        pl.semaphore_signal(barrier, inc=1, device_id=to, device_id_type=MESH)
    pl.semaphore_wait(barrier, 3 + xs + ys + zs - 3)

    def chan_copy(src, dst, ss, rs, to):
        return pltpu.make_async_remote_copy(
            src_ref=src, dst_ref=dst, send_sem=ss, recv_sem=rs, device_id={"chan": to}, device_id_type=MESH
        )

    def right_copy(n, sems, owner, to, src=None):
        place = right.at[n, rows(owner * quarter, quarter), :]
        return chan_copy(place if src is None else src, place, sems[0].at[RIGHT, n], sems[1].at[RIGHT, n], to)

    def left_copy(n, sems, owner, to, src=None):
        place = left.at[n, rows(owner * quarter, quarter), :]
        return chan_copy(place if src is None else src, place, sems[0].at[LEFT, n], sems[1].at[LEFT, n], to)

    sib_sems, par_sems, fwd_sems = (sib_send, sib_recv), (par_send, par_recv), (fwd_send, fwd_recv)
    r_par = [right_copy(n, par_sems, ch, par, r_hbm.at[n]) for n in range(blocks)]
    r_sib = [right_copy(n, sib_sems, ch, sib, r_hbm.at[n]) for n in range(blocks)]
    r_fwd = [right_copy(n, fwd_sems, par, sib) for n in range(blocks)]
    l_par = [left_copy(n, par_sems, ch, par, l_hbm.at[2 * (1 - chip) + n]) for n in range(2)]
    l_sib = [left_copy(n, sib_sems, ch, sib, l_hbm.at[2 * chip + n]) for n in range(2)]
    l_fwd = [left_copy(n, fwd_sems, par, sib) for n in range(2)]
    x_sib = chan_copy(x_hbm, xv.at[:, lanes(SIB)], in_send.at[0], in_recv.at[0], sib)
    b_sib = chan_copy(gated.at[OWN], gated.at[SIB], in_send.at[1], in_recv.at[1], sib)
    for c in r_par + l_par + [x_sib] + r_sib + l_sib:
        c.start()
    for p in y_peers:
        pl.semaphore_signal(row_sem, inc=1, device_id={"seq": p}, device_id_type=MESH)

    def to_piece(r, row, first, count):
        spread[pl.ds(row, count, stride=piece), :] = part[r, pl.ds(first, count, stride=4), :]

    def to_columns(r, local, count):
        for d in range(2):
            to_piece(r, 4 * local + 2 * d + r, 2 * core + d, count)

    def to_positions(r, d):
        for local in range(4):
            to_piece(r, 4 * (2 * d + r) + local, local, n_seq)

    def piece_copy(which, p):
        return pltpu.make_async_remote_copy(
            src_ref=out_s.at[which, rows(p * piece, piece), :],
            dst_ref=out_r.at[which, rows(seq * piece, piece), :],
            send_sem=a2a_send.at[which],
            recv_sem=a2a_recv.at[which],
            device_id={"seq": p, "chan": twist},
            device_id_type=MESH,
        )

    def send_own(which):
        @pl.when(chip == core)
        def _():
            here = rows(seq * piece, piece)
            out_r[which, here, :] = out_s[which, here, :]

        @pl.when(chip != core)
        def _():
            piece_copy(which, seq).start()

    def send_all(which):
        def step(t, carry):
            u = (t * 37) & (n_seq - 1)
            piece_copy(which, seq_of(z + u // (ys * xs), y + u // xs, x + u)).start()
            return carry

        lax.fori_loop(1, n_seq, step, 0)
        send_own(which)

    def send_quarter(which, q):
        def step(t, carry):
            u = (t * 13) & (dests - 1)
            p = q * dests + ((seq + u) & (dests - 1))

            @pl.when(p != seq)
            def _():
                piece_copy(which, p).start()

            return carry

        lax.fori_loop(0, dests, step, 0)

    def wait_pieces(which, sem):
        def wait_for(count):
            ref = out_s.at[which, pl.ds(0, count * piece), :]
            pltpu.make_async_copy(ref, ref, sem.at[which]).wait()

        pl.when(chip == core)(lambda: wait_for(n_seq - 1))
        pl.when(chip != core)(lambda: wait_for(n_seq))

    def share(which):
        return chan_copy(out_r.at[which], sib_r.at[which], share_send.at[which], share_recv.at[which], sib)

    def arrived(which):
        wait_pieces(which, a2a_recv)
        share(which).start()
        flat[OWN] = out_r[which].astype(F32)

    def shared(which):
        share(which).wait_recv()
        flat[SIB] = sib_r[which].astype(F32)

    outs = []

    def put(src, dst, place, which, n):
        outs.append(pltpu.make_async_copy(src.at[place], dst.at[place], out_sem.at[which, n]))
        outs[-1].start()

    loads[0].wait()
    loads[1].wait()
    for n in range(blocks):
        block = pl.ds(n * order, order)
        part[OWN] = yv[block, :].astype(F32) * gv[block, :].astype(F32)
        gated[OWN, block, :] = part[OWN].astype(BF16)
        to_columns(OWN, n, n_seq)
    b_sib.start()
    pl.semaphore_wait(row_sem, ys - 1)
    for p in z_peers:
        pl.semaphore_signal(plane_sem, inc=1, device_id={"seq": p}, device_id_type=MESH)
    b_sib.wait_recv()
    for n in range(blocks):
        part[SIB] = gated[SIB, pl.ds(n * order, order), :].astype(F32)
        to_columns(SIB, n, n_seq)
    out_s[BACK] = spread[...].astype(BF16)
    pl.semaphore_wait(plane_sem, zs - 1)
    send_all(BACK)

    def upper_quarter(q):
        here = pl.ds(0, quarter)
        for n in range(blocks):
            terms = dot(right[n, rows(q * quarter, quarter), :], xv[pl.ds(n * order, order), :])
            for r in range(2):
                part[r, here, :] = terms[:, r * width:(r + 1) * width]
                to_columns(r, n, dests)
        size = dests * piece
        out_s[UPPER, rows(q * size, size), :] = spread[pl.ds(0, size), :].astype(BF16)
        send_quarter(UPPER, q)

    loads[2].wait()
    loads[3].wait()
    x_sib.wait_recv()
    upper_quarter(ch)
    for c in r_sib:
        c.wait_recv()
    upper_quarter(sib)
    for c, f in zip(r_par, r_fwd):
        c.wait_recv()
        f.start()
    upper_quarter(par)
    for f in r_fwd:
        f.wait_recv()
    upper_quarter(ch ^ 3)
    send_own(UPPER)

    for c, f in zip(l_par, l_fwd):
        c.wait_recv()
        f.start()
    loads[4].wait()
    arrived(BACK)
    for c in l_sib + l_fwd:
        c.wait_recv()
    for d in range(2):
        column = [flat[OWN, pl.ds(2 * d + r, order, stride=4), :] for r in range(2)]
        for r in range(2):
            bk[d, :, lanes(r)] = column[r].astype(BF16)
        turned = jnp.concatenate([column[r].T for r in range(2)], axis=0).astype(BF16)
        terms = dot(turned, left[d])
        for r in range(2):
            part[r] = terms[r * width:(r + 1) * width].T
            to_positions(r, d)
    out_s[LOWER] = spread[...].astype(BF16)
    send_all(LOWER)

    arrived(UPPER)
    for d in range(2):
        for r in range(2):
            uk[d, :, lanes(r)] = flat[OWN, pl.ds(2 * d + r, order, stride=4), :].astype(BF16)
        terms = dot(left[d], uk[d, :, pl.ds(0, 2 * width)])
        for r in range(2):
            part[r] = terms[:, r * width:(r + 1) * width]
            to_positions(r, d)
    out_s[MIXED] = spread[...].astype(BF16)
    send_all(MIXED)

    for which, dst in ((BACK, bk), (UPPER, uk)):
        shared(which)
        for d in range(2):
            for r in range(2):
                dst[d, :, lanes(2 + r)] = flat[SIB, pl.ds(2 * d + r, order, stride=4), :].astype(BF16)

    def left_far(d):
        place = grad.at[LEFT, 2 * chip + d]
        return chan_copy(far_l.at[d], place, far_ss.at[LEFT, d], far_rs.at[LEFT, d], par)

    for d in range(2):
        far_l[d] = dot(bk[d, rows(par * quarter, quarter), :], uk[d], ((1,), (1,))).astype(BF16)
        left_far(d).start()

    def right_far(n):
        return chan_copy(far_s.at[n], far_r.at[n], far_ss.at[RIGHT, n], far_rs.at[RIGHT, n], par)

    def right_terms(n, q):
        return dot(lk[n, rows(q * quarter, quarter), :], xv[pl.ds(n * order, order), :], ((1,), (1,)))

    arrived(LOWER)
    shared(LOWER)
    for n in range(blocks):
        for held in (OWN, SIB):
            for d in range(2):
                for r in range(2):
                    part[r, pl.ds(2 * (core ^ held) + d, n_seq, stride=4), :] = (
                        flat[held, pl.ds(4 * (2 * d + (r ^ held)) + n, n_seq, stride=piece), :]
                    )
        for r in range(2):
            lk[n, :, lanes(r)] = part[r].astype(BF16)
        far_s[n] = right_terms(n, par).astype(BF16)
        right_far(n).start()
    for n in range(blocks):
        turned = lk[n, :, lanes(OWN)].astype(F32).T.astype(BF16)
        ig[pl.ds(n * order, order), :] = dot(turned, right[n]).T.astype(BF16)
        put(ig, ig_hbm, pl.ds(n * order, order), 2, n)
    for n in range(blocks):
        home_f[n] = right_terms(n, ch)
    for d in range(2):
        grad[LEFT, 2 * chip + d] = dot(bk[d, rows(ch * quarter, quarter), :], uk[d], ((1,), (1,))).astype(BF16)
        put(grad.at[LEFT], lg_hbm, 2 * chip + d, LEFT, d)

    arrived(MIXED)
    shared(MIXED)
    for n in range(blocks):
        block = pl.ds(n * order, order)
        for held in (OWN, SIB):
            for d in range(2):
                part[0, pl.ds(2 * (core ^ held) + d, n_seq, stride=4), :] = (
                    flat[held, pl.ds(4 * (2 * d + held) + n, n_seq, stride=piece), :]
                )
        gg[block, :] = (yv[block, :].astype(F32) * part[0]).astype(BF16)
        put(gg, gg_hbm, block, 3, n)

    for d in range(2):
        left_far(d).wait_recv()
        put(grad.at[LEFT], lg_hbm, 2 * (1 - chip) + d, LEFT, 2 + d)
    for n in range(blocks):
        right_far(n).wait_recv()
        grad[RIGHT, n] = (home_f[n] + far_r[n].astype(F32)).astype(BF16)
        put(grad.at[RIGHT], rg_hbm, n, RIGHT, n)

    for which in range(4):
        wait_pieces(which, a2a_send)
        share(which).wait_send()
    for c in r_par + r_sib + r_fwd + l_par + l_sib + l_fwd + [x_sib, b_sib]:
        c.wait_send()
    for d in range(2):
        left_far(d).wait_send()
    for n in range(blocks):
        right_far(n).wait_send()
    for c in outs:
        c.wait()


def hand_over(*refs):
    sem = refs[-1]
    copies = [pltpu.make_async_copy(refs[n], refs[4 + n], sem.at[n]) for n in range(4)]
    for c in copies:
        c.start()
    for c in copies:
        c.wait()


def shards(n_seq, inputs, gate, cotangent, right_factor, left_factor):
    tokens, width = inputs.shape
    blocks, quarter, order = right_factor.shape
    piece = 4 * blocks
    data = (tokens, width)
    pieces = (n_seq * piece, width)
    terms = (blocks, quarter, order)
    dma = pltpu.SemaphoreType.DMA
    per_block = dma((2, blocks))
    scratch = (
        [pltpu.VMEM((tokens, 2 * width), BF16)]
        + [pltpu.VMEM(data, BF16)] * 2
        + [pltpu.VMEM((2,) + data, BF16)]
        + [pltpu.VMEM((blocks, order, order), BF16), pltpu.VMEM((2, order, order), BF16)]
        + [pltpu.VMEM((4,) + pieces, BF16)] * 3
        + [pltpu.VMEM((2, order, width), F32), pltpu.VMEM(pieces, F32), pltpu.VMEM((2,) + pieces, F32)]
        + [pltpu.VMEM((2, order, 4 * width), BF16)] * 2
        + [pltpu.VMEM((blocks, order, 2 * width), BF16)]
        + [pltpu.VMEM(data, BF16)] * 2
        + [pltpu.VMEM(terms, BF16)] * 2
        + [pltpu.VMEM((2, quarter, order), BF16), pltpu.VMEM(terms, F32), pltpu.VMEM((2,) + terms, BF16)]
        + [dma((5,))]
        + [dma((4,))] * 4
        + [dma((2,))] * 2
        + [per_block] * 6
        + [per_block] * 2
        + [dma((4, blocks)), pltpu.SemaphoreType.REGULAR, pltpu.SemaphoreType.REGULAR]
    )
    in_hbm = pl.BlockSpec(memory_space=pltpu.HBM)

    given = (inputs, gate, cotangent, right_factor, left_factor)
    results = pl.pallas_call(
        functools.partial(kernel, n_seq),
        out_shape=(
            jax.ShapeDtypeStruct(data, BF16),
            jax.ShapeDtypeStruct(data, BF16),
            jax.ShapeDtypeStruct(right_factor.shape, BF16),
            jax.ShapeDtypeStruct(left_factor.shape, BF16),
        ),
        in_specs=[in_hbm] * 5,
        out_specs=(in_hbm,) * 4,
        scratch_shapes=scratch,
        compiler_params=pltpu.CompilerParams(
            collective_id=0, has_side_effects=True, vmem_limit_bytes=48 * 2**20
        ),
        cost_estimate=pl.CostEstimate(
            flops=12 * blocks * order * order * width, bytes_accessed=9 * 2**19, transcendentals=0
        ),
        name="monarch",
    )(*(pltpu.with_memory_space_constraint(a, pltpu.HBM) for a in given))
    return pl.pallas_call(
        hand_over,
        out_shape=tuple(jax.ShapeDtypeStruct(r.shape, r.dtype) for r in results),
        in_specs=[pl.BlockSpec(memory_space=pltpu.VMEM)] * 4,
        out_specs=(in_hbm,) * 4,
        scratch_shapes=[dma((4,))],
        compiler_params=pltpu.CompilerParams(vmem_limit_bytes=2**20),
        name="hand_over",
    )(*results)


def solution(mesh):
    rows = P("seq", "chan")
    factor = P("seq", "chan", None)
    return jax.shard_map(
        functools.partial(shards, mesh.shape["seq"]),
        mesh=mesh,
        in_specs=(rows, rows, rows, factor, factor),
        out_specs=(rows, rows, factor, factor),
        check_vma=False,
    )
```

```python
import functools

import jax
import jax.numpy as jnp
from jax import lax
from jax.experimental import pallas as pl
from jax.experimental.pallas import tpu as pltpu
from jax.sharding import PartitionSpec as P

MESH = pl.DeviceIdType.MESH
BF16 = jnp.bfloat16
F32 = jnp.float32
UPPER, MIXED, BACK, LOWER = range(4)
RIGHT, LEFT = range(2)
OWN, SIB = range(2)


def torus(n_seq):
    return {128: (8, 4, 4), 8: (2, 2, 2)}[n_seq]


def dot(a, b, dims=((1,), (0,))):
    return lax.dot_general(a, b, (dims, ((), ())), preferred_element_type=F32)


def kernel(
    n_seq,
    x_hbm, g_hbm, y_hbm, r_hbm, l_hbm,
    ig_hbm, gg_hbm, rg_hbm, lg_hbm,
    xv, gv, yv, gated, right, left, out_s, out_r, sib_r, part, spread, flat,
    bk, uk, lk, ig, gg, far_s, far_r, far_l, home_f, grad,
    load_sem, a2a_send, a2a_recv, share_send, share_recv, in_send, in_recv,
    sib_send, sib_recv, par_send, par_recv, fwd_send, fwd_recv,
    far_ss, far_rs, out_sem, row_sem, plane_sem,
):
    zs, ys, xs = torus(n_seq)
    blocks, order, width = right.shape[0], right.shape[1], gv.shape[1]
    quarter = order // 4
    dests = n_seq // 4
    piece = 4 * blocks
    seq, ch = lax.axis_index("seq"), lax.axis_index("chan")
    z, y, x = seq // (ys * xs), (seq // xs) & (ys - 1), seq & (xs - 1)
    chip, core = ch // 2, ch & 1
    sib, par, twist = ch ^ 1, ch ^ 2, 2 * core + chip

    def rows(start, size):
        return pl.ds(pl.multiple_of(start, size), size)

    def lanes(r):
        return pl.ds(r * width, width)

    mine = rows(ch * quarter, quarter)
    loads = [
        pltpu.make_async_copy(src, dst, load_sem.at[n])
        for n, (src, dst) in enumerate((
            (y_hbm, yv), (g_hbm, gv), (r_hbm, right.at[:, mine, :]), (x_hbm, xv.at[:, lanes(OWN)]),
            (l_hbm.at[pl.ds(2 * chip, 2)], left.at[:, mine, :]),
        ))
    ]
    for load in loads:
        load.start()

    def seq_of(a, b, c):
        return (a & (zs - 1)) * (ys * xs) + (b & (ys - 1)) * xs + (c & (xs - 1))

    y_peers = [seq_of(z, y + d, x) for d in range(1, ys)]
    z_peers = [seq_of(z + d, y, x) for d in range(1, zs)]
    barrier = pltpu.get_barrier_semaphore()
    for d in range(1, 4):
        pl.semaphore_signal(barrier, inc=1, device_id={"chan": ch ^ d}, device_id_type=MESH)
    for p in y_peers + z_peers:
        pl.semaphore_signal(barrier, inc=1, device_id={"seq": p}, device_id_type=MESH)
    for d in range(1, xs):
        to = {"seq": seq_of(z, y, x + d), "chan": twist}
        pl.semaphore_signal(barrier, inc=1, device_id=to, device_id_type=MESH)
    pl.semaphore_wait(barrier, 3 + xs + ys + zs - 3)

    def chan_copy(src, dst, ss, rs, to):
        return pltpu.make_async_remote_copy(
            src_ref=src, dst_ref=dst, send_sem=ss, recv_sem=rs, device_id={"chan": to}, device_id_type=MESH
        )

    def right_copy(n, sems, owner, to, src=None):
        place = right.at[n, rows(owner * quarter, quarter), :]
        return chan_copy(place if src is None else src, place, sems[0].at[RIGHT, n], sems[1].at[RIGHT, n], to)

    def left_copy(n, sems, owner, to, src=None):
        place = left.at[n, rows(owner * quarter, quarter), :]
        return chan_copy(place if src is None else src, place, sems[0].at[LEFT, n], sems[1].at[LEFT, n], to)

    sib_sems, par_sems, fwd_sems = (sib_send, sib_recv), (par_send, par_recv), (fwd_send, fwd_recv)
    r_par = [right_copy(n, par_sems, ch, par, r_hbm.at[n]) for n in range(blocks)]
    r_sib = [right_copy(n, sib_sems, ch, sib, r_hbm.at[n]) for n in range(blocks)]
    r_fwd = [right_copy(n, fwd_sems, par, sib) for n in range(blocks)]
    l_par = [left_copy(n, par_sems, ch, par, l_hbm.at[2 * (1 - chip) + n]) for n in range(2)]
    l_sib = [left_copy(n, sib_sems, ch, sib, l_hbm.at[2 * chip + n]) for n in range(2)]
    l_fwd = [left_copy(n, fwd_sems, par, sib) for n in range(2)]
    x_sib = chan_copy(x_hbm, xv.at[:, lanes(SIB)], in_send.at[0], in_recv.at[0], sib)
    b_sib = chan_copy(gated.at[OWN], gated.at[SIB], in_send.at[1], in_recv.at[1], sib)
    for c in r_par + l_par + [x_sib] + r_sib + l_sib:
        c.start()
    for p in y_peers:
        pl.semaphore_signal(row_sem, inc=1, device_id={"seq": p}, device_id_type=MESH)

    def to_piece(r, row, first, count):
        spread[pl.ds(row, count, stride=piece), :] = part[r, pl.ds(first, count, stride=4), :]

    def to_columns(r, local, count):
        for d in range(2):
            to_piece(r, 4 * local + 2 * d + r, 2 * core + d, count)

    def to_positions(r, d):
        for local in range(4):
            to_piece(r, 4 * (2 * d + r) + local, local, n_seq)

    def piece_copy(which, p):
        return pltpu.make_async_remote_copy(
            src_ref=out_s.at[which, rows(p * piece, piece), :],
            dst_ref=out_r.at[which, rows(seq * piece, piece), :],
            send_sem=a2a_send.at[which],
            recv_sem=a2a_recv.at[which],
            device_id={"seq": p, "chan": twist},
            device_id_type=MESH,
        )

    def send_own(which):
        @pl.when(chip == core)
        def _():
            here = rows(seq * piece, piece)
            out_r[which, here, :] = out_s[which, here, :]

        @pl.when(chip != core)
        def _():
            piece_copy(which, seq).start()

    def send_all(which):
        def step(t, carry):
            p = (t * 37) & (n_seq - 1)

            @pl.when(p != seq)
            def _():
                piece_copy(which, p).start()

            return carry

        lax.fori_loop(0, n_seq, step, 0)
        send_own(which)

    def send_quarter(which, q):
        def step(t, carry):
            u = (t * 13) & (dests - 1)
            p = q * dests + ((seq + u) & (dests - 1))

            @pl.when(p != seq)
            def _():
                piece_copy(which, p).start()

            return carry

        lax.fori_loop(0, dests, step, 0)

    def wait_pieces(which, sem):
        def wait_for(count):
            ref = out_s.at[which, pl.ds(0, count * piece), :]
            pltpu.make_async_copy(ref, ref, sem.at[which]).wait()

        pl.when(chip == core)(lambda: wait_for(n_seq - 1))
        pl.when(chip != core)(lambda: wait_for(n_seq))

    def share(which):
        return chan_copy(out_r.at[which], sib_r.at[which], share_send.at[which], share_recv.at[which], sib)

    def arrived(which, held_back=()):
        wait_pieces(which, a2a_recv)
        share(which).start()
        for c in held_back:
            c.start()
        flat[OWN] = out_r[which].astype(F32)

    def shared(which):
        share(which).wait_recv()
        flat[SIB] = sib_r[which].astype(F32)

    outs = []

    def put(src, dst, place, which, n):
        outs.append(pltpu.make_async_copy(src.at[place], dst.at[place], out_sem.at[which, n]))
        outs[-1].start()

    loads[0].wait()
    loads[1].wait()
    for n in range(blocks):
        block = pl.ds(n * order, order)
        part[OWN] = yv[block, :].astype(F32) * gv[block, :].astype(F32)
        gated[OWN, block, :] = part[OWN].astype(BF16)
        to_columns(OWN, n, n_seq)
    b_sib.start()
    pl.semaphore_wait(row_sem, ys - 1)
    for p in z_peers:
        pl.semaphore_signal(plane_sem, inc=1, device_id={"seq": p}, device_id_type=MESH)
    b_sib.wait_recv()
    for n in range(blocks):
        part[SIB] = gated[SIB, pl.ds(n * order, order), :].astype(F32)
        to_columns(SIB, n, n_seq)
    out_s[BACK] = spread[...].astype(BF16)
    pl.semaphore_wait(plane_sem, zs - 1)
    send_all(BACK)

    def upper_quarter(q):
        here = pl.ds(0, quarter)
        for n in range(blocks):
            terms = dot(right[n, rows(q * quarter, quarter), :], xv[pl.ds(n * order, order), :])
            for r in range(2):
                part[r, here, :] = terms[:, r * width:(r + 1) * width]
                to_columns(r, n, dests)
        size = dests * piece
        out_s[UPPER, rows(q * size, size), :] = spread[pl.ds(0, size), :].astype(BF16)
        send_quarter(UPPER, q)

    loads[2].wait()
    loads[3].wait()
    x_sib.wait_recv()
    upper_quarter(ch)
    for c in r_sib:
        c.wait_recv()
    upper_quarter(sib)
    for c, f in zip(r_par, r_fwd):
        c.wait_recv()
        f.start()
    upper_quarter(par)
    for f in r_fwd:
        f.wait_recv()
    upper_quarter(ch ^ 3)
    send_own(UPPER)

    for c, f in zip(l_par, l_fwd):
        c.wait_recv()
        f.start()
    loads[4].wait()
    arrived(BACK)
    for c in l_sib + l_fwd:
        c.wait_recv()
    for d in range(2):
        column = [flat[OWN, pl.ds(2 * d + r, order, stride=4), :] for r in range(2)]
        for r in range(2):
            bk[d, :, lanes(r)] = column[r].astype(BF16)
        turned = jnp.concatenate([column[r].T for r in range(2)], axis=0).astype(BF16)
        terms = dot(turned, left[d])
        for r in range(2):
            part[r] = terms[r * width:(r + 1) * width].T
            to_positions(r, d)
    out_s[LOWER] = spread[...].astype(BF16)
    send_all(LOWER)

    arrived(UPPER)
    for d in range(2):
        for r in range(2):
            uk[d, :, lanes(r)] = flat[OWN, pl.ds(2 * d + r, order, stride=4), :].astype(BF16)
        terms = dot(left[d], uk[d, :, pl.ds(0, 2 * width)])
        for r in range(2):
            part[r] = terms[:, r * width:(r + 1) * width]
            to_positions(r, d)
    out_s[MIXED] = spread[...].astype(BF16)
    send_all(MIXED)

    for which, dst in ((BACK, bk), (UPPER, uk)):
        shared(which)
        for d in range(2):
            for r in range(2):
                dst[d, :, lanes(2 + r)] = flat[SIB, pl.ds(2 * d + r, order, stride=4), :].astype(BF16)

    def left_far(d):
        place = grad.at[LEFT, 2 * chip + d]
        return chan_copy(far_l.at[d], place, far_ss.at[LEFT, d], far_rs.at[LEFT, d], par)

    for d in range(2):
        far_l[d] = dot(bk[d, rows(par * quarter, quarter), :], uk[d], ((1,), (1,))).astype(BF16)
        if d < 1:
            left_far(d).start()

    def right_far(n):
        return chan_copy(far_s.at[n], far_r.at[n], far_ss.at[RIGHT, n], far_rs.at[RIGHT, n], par)

    def right_terms(n, q):
        return dot(lk[n, rows(q * quarter, quarter), :], xv[pl.ds(n * order, order), :], ((1,), (1,)))

    arrived(LOWER, [left_far(1)])
    shared(LOWER)
    for n in range(blocks):
        for held in (OWN, SIB):
            for d in range(2):
                for r in range(2):
                    part[r, pl.ds(2 * (core ^ held) + d, n_seq, stride=4), :] = (
                        flat[held, pl.ds(4 * (2 * d + (r ^ held)) + n, n_seq, stride=piece), :]
                    )
        for r in range(2):
            lk[n, :, lanes(r)] = part[r].astype(BF16)
        far_s[n] = right_terms(n, par).astype(BF16)
        right_far(n).start()
    for n in range(blocks):
        turned = lk[n, :, lanes(OWN)].astype(F32).T.astype(BF16)
        ig[pl.ds(n * order, order), :] = dot(turned, right[n]).T.astype(BF16)
        put(ig, ig_hbm, pl.ds(n * order, order), 2, n)
    for n in range(blocks):
        home_f[n] = right_terms(n, ch)
    for d in range(2):
        grad[LEFT, 2 * chip + d] = dot(bk[d, rows(ch * quarter, quarter), :], uk[d], ((1,), (1,))).astype(BF16)
        put(grad.at[LEFT], lg_hbm, 2 * chip + d, LEFT, d)

    arrived(MIXED)
    shared(MIXED)
    for n in range(blocks):
        block = pl.ds(n * order, order)
        for held in (OWN, SIB):
            for d in range(2):
                part[0, pl.ds(2 * (core ^ held) + d, n_seq, stride=4), :] = (
                    flat[held, pl.ds(4 * (2 * d + held) + n, n_seq, stride=piece), :]
                )
        gg[block, :] = (yv[block, :].astype(F32) * part[0]).astype(BF16)
        put(gg, gg_hbm, block, 3, n)

    for d in range(2):
        left_far(d).wait_recv()
        put(grad.at[LEFT], lg_hbm, 2 * (1 - chip) + d, LEFT, 2 + d)
    for n in range(blocks):
        right_far(n).wait_recv()
        grad[RIGHT, n] = (home_f[n] + far_r[n].astype(F32)).astype(BF16)
        put(grad.at[RIGHT], rg_hbm, n, RIGHT, n)

    for which in range(4):
        wait_pieces(which, a2a_send)
        share(which).wait_send()
    for c in r_par + r_sib + r_fwd + l_par + l_sib + l_fwd + [x_sib, b_sib]:
        c.wait_send()
    for d in range(2):
        left_far(d).wait_send()
    for n in range(blocks):
        right_far(n).wait_send()
    for c in outs:
        c.wait()


def hand_over(*refs):
    sem = refs[-1]
    copies = [pltpu.make_async_copy(refs[n], refs[4 + n], sem.at[n]) for n in range(4)]
    for c in copies:
        c.start()
    for c in copies:
        c.wait()


def shards(n_seq, inputs, gate, cotangent, right_factor, left_factor):
    tokens, width = inputs.shape
    blocks, quarter, order = right_factor.shape
    piece = 4 * blocks
    data = (tokens, width)
    pieces = (n_seq * piece, width)
    terms = (blocks, quarter, order)
    dma = pltpu.SemaphoreType.DMA
    per_block = dma((2, blocks))
    scratch = (
        [pltpu.VMEM((tokens, 2 * width), BF16)]
        + [pltpu.VMEM(data, BF16)] * 2
        + [pltpu.VMEM((2,) + data, BF16)]
        + [pltpu.VMEM((blocks, order, order), BF16), pltpu.VMEM((2, order, order), BF16)]
        + [pltpu.VMEM((4,) + pieces, BF16)] * 3
        + [pltpu.VMEM((2, order, width), F32), pltpu.VMEM(pieces, F32), pltpu.VMEM((2,) + pieces, F32)]
        + [pltpu.VMEM((2, order, 4 * width), BF16)] * 2
        + [pltpu.VMEM((blocks, order, 2 * width), BF16)]
        + [pltpu.VMEM(data, BF16)] * 2
        + [pltpu.VMEM(terms, BF16)] * 2
        + [pltpu.VMEM((2, quarter, order), BF16), pltpu.VMEM(terms, F32), pltpu.VMEM((2,) + terms, BF16)]
        + [dma((5,))]
        + [dma((4,))] * 4
        + [dma((2,))] * 2
        + [per_block] * 6
        + [per_block] * 2
        + [dma((4, blocks)), pltpu.SemaphoreType.REGULAR, pltpu.SemaphoreType.REGULAR]
    )
    in_hbm = pl.BlockSpec(memory_space=pltpu.HBM)

    given = (inputs, gate, cotangent, right_factor, left_factor)
    results = pl.pallas_call(
        functools.partial(kernel, n_seq),
        out_shape=(
            jax.ShapeDtypeStruct(data, BF16),
            jax.ShapeDtypeStruct(data, BF16),
            jax.ShapeDtypeStruct(right_factor.shape, BF16),
            jax.ShapeDtypeStruct(left_factor.shape, BF16),
        ),
        in_specs=[in_hbm] * 5,
        out_specs=(in_hbm,) * 4,
        scratch_shapes=scratch,
        compiler_params=pltpu.CompilerParams(
            collective_id=0, has_side_effects=True, vmem_limit_bytes=48 * 2**20
        ),
        cost_estimate=pl.CostEstimate(
            flops=12 * blocks * order * order * width, bytes_accessed=9 * 2**19, transcendentals=0
        ),
        name="monarch",
    )(*(pltpu.with_memory_space_constraint(a, pltpu.HBM) for a in given))
    return pl.pallas_call(
        hand_over,
        out_shape=tuple(jax.ShapeDtypeStruct(r.shape, r.dtype) for r in results),
        in_specs=[pl.BlockSpec(memory_space=pltpu.VMEM)] * 4,
        out_specs=(in_hbm,) * 4,
        scratch_shapes=[dma((4,))],
        compiler_params=pltpu.CompilerParams(vmem_limit_bytes=2**20),
        name="hand_over",
    )(*results)


def solution(mesh):
    rows = P("seq", "chan")
    factor = P("seq", "chan", None)
    return jax.shard_map(
        functools.partial(shards, mesh.shape["seq"]),
        mesh=mesh,
        in_specs=(rows, rows, rows, factor, factor),
        out_specs=(rows, rows, factor, factor),
        check_vma=False,
    )
```
